512 devices in a mesh: vox: 16 (over y, z_hi), feat: 32 (over x, z_lo, core).
Axes of the slice: x: 4, y: 4, z: 16 (z_hi: 4, z_lo: 4; z = z_hi * 4 + z_lo), core: 2. Of those that a mesh axis runs over, the one named last changes fastest.
Arguments:
- hidden_states: bfloat16 [8192, 8192], P('vox', 'feat'), may hold values from -6 to 6
- measured_signals: bfloat16 [8192, 2048], P('feat', 'vox'), may hold values from -6 to 6
- spectral_directions: bfloat16 [8192, 8192], P('feat'), may hold values from -0.0625 to 0.0625
- spectral_strengths: float32 [8192], replicated, may hold values from 0.002 to 0.02
- shrinkage_strengths: float32 [16], replicated, may hold values from 0.001 to 0.01
- chosen_shrinkage_slot: int32 [2048], P('vox'), may hold values from 0 to 15
Outputs:
- encoding: float32 [8192, 2048], P('feat', 'vox')
The draws below stay inside these ranges and needn't reach their ends.
All inputs are finite; a program needn't handle non-finite values.
Results may differ from the reference program's by a relative error of at most 0.0036.
Values may be sent and summed in bfloat16 or wider, within the bound.
No kernel may reach another device: no remote copies, remote signals or barrier semaphores. Data moves between devices by JAX's collectives and lax.ppermute only.
A program may use at most 64 MiB of HBM per device.

```python
import math
import jax
import jax.numpy as jnp

D = 8192
SHRINKAGE_LEVELS = 16
TR = 8192
VOXELS = 2048


def set_ends(array, rng, smallest, top_value):
    spot = [jax.random.randint(jax.random.fold_in(rng, axis), (), 0, length) for axis, length in enumerate(array.shape)]
    main_axis = array.shape.index(max(array.shape))
    neighbour = spot[:main_axis] + [(spot[main_axis] + 1) % array.shape[main_axis]] + spot[main_axis + 1:]
    return array.at[tuple(spot)].set(smallest).at[tuple(neighbour)].set(top_value)


def block_levels(rng, dims, pieces, low, top_value):
    gain = 1.0
    for dim, blocks in pieces:
        heights = jax.random.uniform(jax.random.fold_in(jax.random.fold_in(rng, 6), dim), (blocks,), jnp.float32, low / len(pieces), top_value / len(pieces))
        gain = gain * jnp.repeat(jnp.exp(heights), dims[dim] // blocks).reshape((-1,) + (1,) * (len(dims) - 1 - dim))
    return gain


def scatter_about(stream_key, shape, scale, reach, pieces=(), dtype=jnp.bfloat16):
    values = jax.random.normal(stream_key, shape, jnp.float32) * scale
    if len(pieces) > 0:
        values = block_levels(stream_key, shape, pieces, -0.22, 0.18) * values
    return jnp.clip(values, min=-reach, max=reach).astype(dtype)


def setup_inputs(seed: int = 0) -> dict:
    key_of = jax.random.split(jax.random.key(seed), 7)
    hidden_states = scatter_about(key_of[0], (TR, D), 1.0, 6.0, ((0, 16), (1, 32)))
    measured_signals = scatter_about(key_of[1], (TR, VOXELS), 1.0, 6.0, ((0, 32), (1, 16)))
    spectral_directions = scatter_about(key_of[2], (D, D), D ** -0.5, 0.0625, ((0, 32),))
    spectral_strengths = jnp.clip(jnp.exp(jax.random.uniform(key_of[3], (D,), jnp.float32, math.log(0.002), math.log(0.02))), 0.002, 0.02)
    shrinkage_strengths = jnp.clip(jnp.exp(jax.random.uniform(key_of[4], (SHRINKAGE_LEVELS,), jnp.float32, math.log(0.001), math.log(0.01))), 0.001, 0.01)
    chosen_shrinkage_slot = set_ends(jax.random.randint(key_of[5], (VOXELS,), 0, SHRINKAGE_LEVELS), jax.random.fold_in(key_of[5], 1), 0, SHRINKAGE_LEVELS - 1).astype(jnp.int32)
    return {"hidden_states": hidden_states, "measured_signals": measured_signals, "spectral_directions": spectral_directions, "spectral_strengths": spectral_strengths, "shrinkage_strengths": shrinkage_strengths, "chosen_shrinkage_slot": chosen_shrinkage_slot}


def reference(hidden_states, measured_signals, spectral_directions, spectral_strengths, shrinkage_strengths, chosen_shrinkage_slot):
    covariance = (jnp.dot(hidden_states.T, measured_signals, preferred_element_type=jnp.float32) / TR).astype(jnp.bfloat16)
    eigen_rotated = jnp.dot(spectral_directions.T, covariance, preferred_element_type=jnp.float32)
    fitted_coefficients = shrinkage_strengths[chosen_shrinkage_slot]
    shrunk = (eigen_rotated / (spectral_strengths[:, None] + fitted_coefficients[None, :])).astype(jnp.bfloat16)
    return jnp.dot(spectral_directions, shrunk, preferred_element_type=jnp.float32)
```

```python
import jax
import jax.numpy as jnp
from jax import lax
from jax.sharding import Mesh, PartitionSpec as P


def exchange(blocks, axis):
    return lax.all_to_all(blocks, axis, 0, 0, tiled=True)


def gather(block, axis, size):
    blocks = jnp.broadcast_to(block[None], (size,) + block.shape)
    return exchange(blocks, axis)


def per_device(
    hidden_states,
    measured_signals,
    spectral_directions,
    spectral_strengths,
    shrinkage_strengths,
    chosen_shrinkage_slot,
):
    f32, bf16 = jnp.float32, jnp.bfloat16
    ny, nzh, nx, nzl, nc = (lax.axis_size(a) for a in ("y", "zh", "x", "zl", "core"))
    rows, width = spectral_directions.shape
    total_time = hidden_states.shape[0] * ny * nzh
    block, voxels = measured_signals.shape

    features = lax.all_gather(hidden_states, "y", axis=0, tiled=False)

    swap = [(a * nzl + b, b * nzl + a) for a in range(nzh) for b in range(nzl)]
    signals = lax.ppermute(measured_signals, ("zh", "zl"), swap)
    signals = gather(signals, "zl", nzl)
    signals = gather(signals, "x", nx)
    signals = gather(signals, "core", nc)

    features = features.reshape(ny, nc, block, rows)
    cross = jnp.einsum("ycta,cygtv->gav", features, signals, preferred_element_type=f32)
    cross = jnp.sum(
        exchange(cross.reshape(nzh, rows, voxels), "zh").reshape(nzh, rows, voxels), axis=0
    )
    covariance = (cross / total_time).astype(bf16)

    slots = jnp.arange(shrinkage_strengths.shape[0], dtype=jnp.int32)
    mask = (chosen_shrinkage_slot[:, None] == slots[None, :]).astype(f32)
    ridge = jnp.sum(mask * shrinkage_strengths[None, :], axis=1)

    rotated = lax.dot_general(
        covariance, spectral_directions, (((0,), (0,)), ((), ())), preferred_element_type=f32
    )
    rotated = rotated.reshape(voxels, nc, width // nc)
    core = lax.axis_index("core")
    mine = lax.dynamic_index_in_dim(rotated, core, 1, keepdims=False)
    other = lax.dynamic_index_in_dim(rotated, 1 - core, 1, keepdims=False)
    rotated = mine + lax.ppermute(other, "core", [(0, 1), (1, 0)])

    def scatter(values, axis, size):
        parts = values.astype(bf16).reshape(voxels, size, values.shape[1] // size)
        parts = exchange(parts.transpose(1, 0, 2), axis)
        return jnp.sum(parts.astype(f32), axis=0)

    rotated = scatter(rotated, "x", nx)
    rotated = scatter(rotated, "zl", nzl)
    share = rotated.shape[1]
    index = (core * nx + lax.axis_index("x")) * nzl + lax.axis_index("zl")
    strengths = lax.dynamic_slice_in_dim(spectral_strengths, index * share, share)
    shrunk = (rotated / (strengths[None, :] + ridge[:, None])).astype(bf16).T

    shrunk = gather(shrunk, "zl", nzl)
    shrunk = gather(shrunk, "x", nx)
    shrunk = gather(shrunk, "core", nc)
    shrunk = shrunk.reshape(width, voxels)
    return jnp.dot(spectral_directions, shrunk, preferred_element_type=f32)


def solution(mesh):
    fine = Mesh(mesh.devices.reshape(4, 4, 4, 4, 2), ("y", "zh", "x", "zl", "core"))
    vox, feat = ("y", "zh"), ("x", "zl", "core")
    return jax.shard_map(
        per_device,
        mesh=fine,
        in_specs=(P(vox, feat), P(feat, vox), P(feat, None), P(), P(), P(vox)),
        out_specs=P(feat, vox),
        check_vma=False,
    )
```

```python
import functools

import jax
import jax.numpy as jnp
from jax import lax
from jax.experimental import pallas as pl
from jax.experimental.pallas import tpu as pltpu
from jax.sharding import Mesh, PartitionSpec as P

F32, BF16, F16 = jnp.float32, jnp.bfloat16, jnp.float16
STEPS = (64, 32, 16, 8, 4, 2, 1)
EXTRA = 16


def exchange(blocks, axis):
    return lax.all_to_all(blocks, axis, 0, 0, tiled=True)


def gather(block, axis, size):
    return exchange(jnp.broadcast_to(block[None], (size,) + block.shape), axis)


def shift(block, axis, size, by):
    return lax.ppermute(block, axis, [(i, (i + by) % size) for i in range(size)])


def whole(count):
    return [pl.BlockSpec(memory_space=pltpu.VMEM)] * count


def cross_kernel(ny, block, first, where, *refs):
    features, signals, total, out = refs[:ny], refs[ny], refs[-2], refs[-1]
    start = pl.multiple_of(where[1] * block, block)
    groups, voxels, _ = signals.shape[1:]
    acc = None if first else total[...]
    for k in range(ny):
        other = lax.rem(where[0] - k + ny, ny)
        left = signals[other].reshape(groups * voxels, block)
        right = features[k][pl.ds(start, block), :]
        term = jnp.dot(left, right, preferred_element_type=F32)
        acc = term if acc is None else acc + term
    if first:
        out[...] = acc
        return
    acc = acc * (1.0 / (ny * groups * 2 * block))
    top = jnp.max(jnp.max(jnp.abs(acc), axis=0, keepdims=True), axis=1, keepdims=True)
    scale, exponent = jnp.ones_like(top), jnp.zeros_like(top)
    for step in STEPS:
        grown = scale * 2.0**step
        fits = top * grown < 2.0**14
        scale = jnp.where(fits, grown, scale)
        exponent = jnp.where(fits, exponent + step, exponent)
    out[:, :voxels, :] = (acc * scale).reshape(groups, voxels, -1)
    out[:, voxels:, :] = jnp.broadcast_to(exponent[None], (groups, EXTRA, acc.shape[1]))


def cross_products(where, features, signals, total):
    ny, (time, rows) = len(features), features[0].shape
    _, groups, voxels, block = signals.shape
    first = total is None
    operands = list(features) + [signals] + ([] if first else [total])
    shape = (groups * voxels, rows) if first else (groups, voxels + EXTRA, rows)
    return pl.pallas_call(
        functools.partial(cross_kernel, ny, block, first),
        out_shape=jax.ShapeDtypeStruct(shape, F32),
        in_specs=[pl.BlockSpec(memory_space=pltpu.SMEM)] + whole(len(operands)),
        out_specs=pl.BlockSpec(memory_space=pltpu.VMEM),
        compiler_params=pltpu.CompilerParams(vmem_limit_bytes=16 << 20),
        cost_estimate=pl.CostEstimate(
            flops=2 * ny * block * groups * voxels * rows, bytes_accessed=4 << 20, transcendentals=0
        ),
    )(where, *operands)


def covariance_kernel(parts, out):
    voxels = out.shape[0]
    total = None
    for k in range(parts.shape[0]):
        exponent = parts[k, voxels : voxels + 1, :]
        scale = jnp.ones_like(exponent)
        for step in STEPS:
            holds = exponent >= step
            scale = jnp.where(holds, scale * 0.5**step, scale)
            exponent = jnp.where(holds, exponent - step, exponent)
        term = parts[k, :voxels, :] * scale
        total = term if total is None else total + term
    out[...] = total.astype(out.dtype)


def rounded_covariance(parts):
    count, rows, width = parts.shape
    return pl.pallas_call(
        covariance_kernel,
        out_shape=jax.ShapeDtypeStruct((rows - EXTRA, width), BF16),
        in_specs=whole(1),
        out_specs=pl.BlockSpec(memory_space=pltpu.VMEM),
        compiler_params=pltpu.CompilerParams(vmem_limit_bytes=16 << 20),
        cost_estimate=pl.CostEstimate(
            flops=2 * parts.size, bytes_accessed=4 * parts.size, transcendentals=0
        ),
    )(parts)


def rotate_kernel(half, own, directions, theirs, their_directions, out):
    product = jnp.dot(own[...], directions[...], preferred_element_type=F32)
    product += jnp.dot(theirs[...], their_directions[...], preferred_element_type=F32)
    share = out.shape[-1]
    for j in range(out.shape[1]):
        out[0, j] = product[:, j * share : (j + 1) * share].astype(out.dtype)


def rotate(half, own, directions, theirs, their_directions, nx, nzl):
    voxels, rows = own.shape
    columns = their_directions.shape[1] // nx
    share = columns // nzl
    flat = pl.BlockSpec((voxels, rows), lambda i, h: (0, 0))
    return pl.pallas_call(
        rotate_kernel,
        out_shape=jax.ShapeDtypeStruct((nx, nzl, voxels, share), BF16),
        grid_spec=pltpu.PrefetchScalarGridSpec(
            num_scalar_prefetch=1,
            grid=(nx,),
            in_specs=[
                flat,
                pl.BlockSpec((rows, columns), lambda i, h: (0, h[0] * nx + i)),
                flat,
                pl.BlockSpec((rows, columns), lambda i, h: (0, i)),
            ],
            out_specs=pl.BlockSpec((1, nzl, voxels, share), lambda i, h: (i, 0, 0, 0)),
        ),
        compiler_params=pltpu.CompilerParams(vmem_limit_bytes=16 << 20),
        cost_estimate=pl.CostEstimate(
            flops=4 * rows * columns * nx * voxels, bytes_accessed=4 << 20, transcendentals=0
        ),
    )(half, own, directions, theirs, their_directions)


def add_kernel(parts, out):
    out[...] = jnp.sum(parts[...].astype(F32), axis=0).astype(out.dtype)


def add_parts(parts):
    return pl.pallas_call(
        add_kernel,
        out_shape=jax.ShapeDtypeStruct(parts.shape[1:], BF16),
        in_specs=whole(1),
        out_specs=pl.BlockSpec(memory_space=pltpu.VMEM),
        compiler_params=pltpu.CompilerParams(vmem_limit_bytes=16 << 20),
        cost_estimate=pl.CostEstimate(
            flops=parts.size, bytes_accessed=3 * parts.size, transcendentals=0
        ),
    )(parts)


def shrink_kernel(levels, which, parts, strengths, slots, grid_values, out):
    voxels = slots.shape[1]
    ridge = jnp.zeros((1, voxels), F32)
    for level in range(levels):
        ridge = jnp.where(slots[...] == level, grid_values[level], ridge)
    column = jnp.broadcast_to(ridge, (voxels, voxels)).T
    rotated = jnp.sum(parts[...].astype(F32), axis=0)
    for j in range(0, out.shape[0], voxels):
        denominator = strengths[0, :, j : j + voxels] + column
        out[j : j + voxels, :] = (rotated[:, j : j + voxels] / denominator).T.astype(out.dtype)


def shrink(which, parts, strengths, grid_values, slots):
    _, voxels, share = parts.shape
    levels = grid_values.shape[0]
    return pl.pallas_call(
        functools.partial(shrink_kernel, levels),
        out_shape=jax.ShapeDtypeStruct((share, voxels), BF16),
        grid_spec=pltpu.PrefetchScalarGridSpec(
            num_scalar_prefetch=1,
            grid=(1,),
            in_specs=[
                pl.BlockSpec(parts.shape, lambda i, w: (0, 0, 0)),
                pl.BlockSpec((1, 1, share), lambda i, w: (w[0], 0, 0)),
                pl.BlockSpec((1, voxels), lambda i, w: (0, 0)),
                pl.BlockSpec(memory_space=pltpu.SMEM),
            ],
            out_specs=pl.BlockSpec((share, voxels), lambda i, w: (0, 0)),
        ),
        compiler_params=pltpu.CompilerParams(vmem_limit_bytes=16 << 20),
        cost_estimate=pl.CostEstimate(
            flops=6 * parts.size, bytes_accessed=2 * parts.size, transcendentals=0
        ),
    )(which, parts, strengths.reshape(-1, 1, share), slots.reshape(1, voxels), grid_values)


def encode_kernel(half, directions, shrunk, out):
    @pl.when(pl.program_id(0) == 0)
    def _():
        out[...] = jnp.zeros_like(out)

    out[...] += jnp.dot(directions[...], shrunk[...], preferred_element_type=F32)


def encode(half, directions, shrunk, steps=4):
    rows, _ = directions.shape
    depth, voxels = shrunk.shape
    columns = depth // steps
    return pl.pallas_call(
        encode_kernel,
        out_shape=jax.ShapeDtypeStruct((rows, voxels), F32),
        grid_spec=pltpu.PrefetchScalarGridSpec(
            num_scalar_prefetch=1,
            grid=(steps,),
            in_specs=[
                pl.BlockSpec((rows, columns), lambda i, h: (0, h[0] * steps + i)),
                pl.BlockSpec((columns, voxels), lambda i, h: (i, 0)),
            ],
            out_specs=pl.BlockSpec((rows, voxels), lambda i, h: (0, 0)),
        ),
        compiler_params=pltpu.CompilerParams(vmem_limit_bytes=16 << 20),
        cost_estimate=pl.CostEstimate(
            flops=2 * rows * depth * voxels, bytes_accessed=4 << 20, transcendentals=0
        ),
    )(half, directions, shrunk)


def per_device(
    hidden_states,
    measured_signals,
    spectral_directions,
    spectral_strengths,
    shrinkage_strengths,
    chosen_shrinkage_slot,
):
    ny, nzh, nx, nzl = (lax.axis_size(a) for a in ("y", "zh", "x", "zl"))
    width = spectral_directions.shape[1]
    core = lax.axis_index("core")
    mine, other = core.reshape(1), (1 - core).reshape(1)
    y = lax.axis_index("y").reshape(1)

    swap = [(a * nzl + b, b * nzl + a) for a in range(nzh) for b in range(nzl)]
    signals = lax.ppermute(measured_signals.T, ("zh", "zl"), swap)
    given = lax.dynamic_slice_in_dim(spectral_directions, (1 - core) * (width // 2), width // 2, axis=1)
    features = [hidden_states] + [shift(hidden_states, "y", ny, k) for k in range(1, ny)]
    signals, given = lax.optimization_barrier((signals, given))
    signals = gather(signals, "zl", nzl)
    signals = gather(signals, "x", nx)
    signals, *features = lax.optimization_barrier((signals, *features))
    signals_other = shift(signals, "core", 2, 1)
    cross = cross_products(jnp.concatenate([y, mine]), features, signals, None)
    cross = cross_products(jnp.concatenate([y, other]), features, signals_other, cross)
    cross, given = lax.optimization_barrier((cross, given))
    their_directions = shift(given, "core", 2, 1)
    parts = exchange(cross.astype(F16), "zh").astype(F32)
    parts, their_directions = lax.optimization_barrier((parts, their_directions))

    covariance = rounded_covariance(parts)
    their_covariance = shift(covariance, "core", 2, 1)
    rotated = rotate(
        mine, covariance, spectral_directions, their_covariance, their_directions, nx, nzl
    )
    rotated = exchange(rotated, "x")
    rotated = exchange(add_parts(rotated), "zl")
    index = (core * nx + lax.axis_index("x")) * nzl + lax.axis_index("zl")
    shrunk = shrink(
        index.reshape(1), rotated, spectral_strengths, shrinkage_strengths, chosen_shrinkage_slot
    )

    shrunk = gather(shrunk, "zl", nzl)
    shrunk = gather(shrunk, "x", nx).reshape(width // 2, -1)
    theirs = encode(jnp.zeros((1,), jnp.int32), their_directions, shrunk)
    received = shift(theirs, "core", 2, 1)
    return encode(mine, spectral_directions, shrunk) + received


def solution(mesh):
    fine = Mesh(mesh.devices.reshape(4, 4, 4, 4, 2), ("y", "zh", "x", "zl", "core"))
    vox, feat = ("y", "zh"), ("x", "zl", "core")
    return jax.shard_map(
        per_device,
        mesh=fine,
        in_specs=(P(vox, feat), P(feat, vox), P(feat, None), P(), P(), P(vox)),
        out_specs=P(feat, vox),
        check_vma=False,
    )
```

```python
import functools

import jax
import jax.numpy as jnp
from jax import lax
from jax.experimental import pallas as pl
from jax.experimental.pallas import tpu as pltpu
from jax.sharding import Mesh, PartitionSpec as P

F32, BF16, F16 = jnp.float32, jnp.bfloat16, jnp.float16
STEPS = (64, 32, 16, 8, 4, 2, 1)
EXTRA = 16


def exchange(blocks, axis):
    return lax.all_to_all(blocks, axis, 0, 0, tiled=True)


def gather(block, axis, size):
    return exchange(jnp.broadcast_to(block[None], (size,) + block.shape), axis)


def shift(block, axis, size, by):
    return lax.ppermute(block, axis, [(i, (i + by) % size) for i in range(size)])


def whole(count):
    return [pl.BlockSpec(memory_space=pltpu.VMEM)] * count


def cross_kernel(ny, which, y, signals, *refs):
    features, out = refs[:ny], refs[ny]
    groups, voxels, block = signals.shape[1:]
    acc = None
    for k in range(ny):
        left = signals[lax.rem(y[0] - k + ny, ny)].reshape(groups * voxels, block)
        term = jnp.dot(left, features[k][which], preferred_element_type=F32)
        acc = term if acc is None else acc + term
    out[...] = acc


def cross_products(which, y, signals, features):
    ny, (_, block, rows) = len(features), features[0].shape
    _, groups, voxels, _ = signals.shape
    return pl.pallas_call(
        functools.partial(cross_kernel, ny, which),
        out_shape=jax.ShapeDtypeStruct((groups * voxels, rows), F32),
        in_specs=[pl.BlockSpec(memory_space=pltpu.SMEM)] + whole(1 + ny),
        out_specs=pl.BlockSpec(memory_space=pltpu.VMEM),
        compiler_params=pltpu.CompilerParams(vmem_limit_bytes=16 << 20),
        cost_estimate=pl.CostEstimate(
            flops=2 * ny * block * groups * voxels * rows, bytes_accessed=4 << 20, transcendentals=0
        ),
    )(y, signals, *features)


def scale_kernel(total_time, kept, received, out):
    groups, voxels = out.shape[0], out.shape[1] - EXTRA
    acc = (kept[...] + received[...]) * (1.0 / total_time)
    top = jnp.max(jnp.max(jnp.abs(acc), axis=0, keepdims=True), axis=1, keepdims=True)
    scale, exponent = jnp.ones_like(top), jnp.zeros_like(top)
    for step in STEPS:
        grown = scale * 2.0**step
        fits = top * grown < 2.0**14
        scale = jnp.where(fits, grown, scale)
        exponent = jnp.where(fits, exponent + step, exponent)
    out[:, :voxels, :] = (acc * scale).reshape(groups, voxels, -1)
    out[:, voxels:, :] = jnp.broadcast_to(exponent[None], (groups, EXTRA, acc.shape[1]))


def scaled(kept, received, groups, total_time):
    rows, width = kept.shape
    return pl.pallas_call(
        functools.partial(scale_kernel, total_time),
        out_shape=jax.ShapeDtypeStruct((groups, rows // groups + EXTRA, width), F32),
        in_specs=whole(2),
        out_specs=pl.BlockSpec(memory_space=pltpu.VMEM),
        compiler_params=pltpu.CompilerParams(vmem_limit_bytes=16 << 20),
        cost_estimate=pl.CostEstimate(
            flops=5 * kept.size, bytes_accessed=12 * kept.size, transcendentals=0
        ),
    )(kept, received)


def covariance_kernel(parts, out):
    voxels = out.shape[0]
    total = None
    for k in range(parts.shape[0]):
        exponent = parts[k, voxels : voxels + 1, :]
        scale = jnp.ones_like(exponent)
        for step in STEPS:
            holds = exponent >= step
            scale = jnp.where(holds, scale * 0.5**step, scale)
            exponent = jnp.where(holds, exponent - step, exponent)
        term = parts[k, :voxels, :] * scale
        total = term if total is None else total + term
    out[...] = total.astype(out.dtype)


def rounded_covariance(parts):
    count, rows, width = parts.shape
    return pl.pallas_call(
        covariance_kernel,
        out_shape=jax.ShapeDtypeStruct((rows - EXTRA, width), BF16),
        in_specs=whole(1),
        out_specs=pl.BlockSpec(memory_space=pltpu.VMEM),
        compiler_params=pltpu.CompilerParams(vmem_limit_bytes=16 << 20),
        cost_estimate=pl.CostEstimate(
            flops=2 * parts.size, bytes_accessed=4 * parts.size, transcendentals=0
        ),
    )(parts)


def rotate_kernel(half, covariances, directions, their_directions, out):
    own, theirs = covariances[half[0]], covariances[1 - half[0]]
    product = jnp.dot(own, directions[...], preferred_element_type=F32)
    product += jnp.dot(theirs, their_directions[...], preferred_element_type=F32)
    share = out.shape[-1]
    for j in range(out.shape[1]):
        out[0, j] = product[:, j * share : (j + 1) * share].astype(out.dtype)


def rotate(half, covariances, directions, their_directions, nx, nzl):
    _, voxels, rows = covariances.shape
    columns = their_directions.shape[1] // nx
    share = columns // nzl
    return pl.pallas_call(
        rotate_kernel,
        out_shape=jax.ShapeDtypeStruct((nx, nzl, voxels, share), BF16),
        grid_spec=pltpu.PrefetchScalarGridSpec(
            num_scalar_prefetch=1,
            grid=(nx,),
            in_specs=[
                pl.BlockSpec(covariances.shape, lambda i, h: (0, 0, 0)),
                pl.BlockSpec((rows, columns), lambda i, h: (0, h[0] * nx + i)),
                pl.BlockSpec((rows, columns), lambda i, h: (0, i)),
            ],
            out_specs=pl.BlockSpec((1, nzl, voxels, share), lambda i, h: (i, 0, 0, 0)),
        ),
        compiler_params=pltpu.CompilerParams(vmem_limit_bytes=16 << 20),
        cost_estimate=pl.CostEstimate(
            flops=4 * rows * columns * nx * voxels, bytes_accessed=4 << 20, transcendentals=0
        ),
    )(half, covariances, directions, their_directions)


def add_kernel(parts, out):
    out[...] = jnp.sum(parts[...].astype(F32), axis=0).astype(out.dtype)


def add_parts(parts):
    return pl.pallas_call(
        add_kernel,
        out_shape=jax.ShapeDtypeStruct(parts.shape[1:], BF16),
        in_specs=whole(1),
        out_specs=pl.BlockSpec(memory_space=pltpu.VMEM),
        compiler_params=pltpu.CompilerParams(vmem_limit_bytes=16 << 20),
        cost_estimate=pl.CostEstimate(
            flops=parts.size, bytes_accessed=3 * parts.size, transcendentals=0
        ),
    )(parts)


def shrink_kernel(levels, which, parts, strengths, slots, grid_values, out):
    voxels = slots.shape[1]
    ridge = jnp.zeros((1, voxels), F32)
    for level in range(levels):
        ridge = jnp.where(slots[...] == level, grid_values[level], ridge)
    column = jnp.broadcast_to(ridge, (voxels, voxels)).T
    rotated = jnp.sum(parts[...].astype(F32), axis=0)
    for j in range(0, out.shape[0], voxels):
        denominator = strengths[0, :, j : j + voxels] + column
        out[j : j + voxels, :] = (rotated[:, j : j + voxels] / denominator).T.astype(out.dtype)


def shrink(which, parts, strengths, grid_values, slots):
    _, voxels, share = parts.shape
    levels = grid_values.shape[0]
    return pl.pallas_call(
        functools.partial(shrink_kernel, levels),
        out_shape=jax.ShapeDtypeStruct((share, voxels), BF16),
        grid_spec=pltpu.PrefetchScalarGridSpec(
            num_scalar_prefetch=1,
            grid=(1,),
            in_specs=[
                pl.BlockSpec(parts.shape, lambda i, w: (0, 0, 0)),
                pl.BlockSpec((1, 1, share), lambda i, w: (w[0], 0, 0)),
                pl.BlockSpec((1, voxels), lambda i, w: (0, 0)),
                pl.BlockSpec(memory_space=pltpu.SMEM),
            ],
            out_specs=pl.BlockSpec((share, voxels), lambda i, w: (0, 0)),
        ),
        compiler_params=pltpu.CompilerParams(vmem_limit_bytes=16 << 20),
        cost_estimate=pl.CostEstimate(
            flops=6 * parts.size, bytes_accessed=2 * parts.size, transcendentals=0
        ),
    )(which, parts, strengths.reshape(-1, 1, share), slots.reshape(1, voxels), grid_values)


def encode_kernel(half, directions, shrunk, out):
    @pl.when(pl.program_id(0) == 0)
    def _():
        out[...] = jnp.zeros_like(out)

    out[...] += jnp.dot(directions[...], shrunk[...], preferred_element_type=F32)


def encode(half, directions, shrunk, steps=4):
    rows, _ = directions.shape
    depth, voxels = shrunk.shape
    columns = depth // steps
    return pl.pallas_call(
        encode_kernel,
        out_shape=jax.ShapeDtypeStruct((rows, voxels), F32),
        grid_spec=pltpu.PrefetchScalarGridSpec(
            num_scalar_prefetch=1,
            grid=(steps,),
            in_specs=[
                pl.BlockSpec((rows, columns), lambda i, h: (0, h[0] * steps + i)),
                pl.BlockSpec((columns, voxels), lambda i, h: (i, 0)),
            ],
            out_specs=pl.BlockSpec((rows, voxels), lambda i, h: (0, 0)),
        ),
        compiler_params=pltpu.CompilerParams(vmem_limit_bytes=16 << 20),
        cost_estimate=pl.CostEstimate(
            flops=2 * rows * depth * voxels, bytes_accessed=4 << 20, transcendentals=0
        ),
    )(half, directions, shrunk)


def per_device(
    hidden_states,
    measured_signals,
    spectral_directions,
    spectral_strengths,
    shrinkage_strengths,
    chosen_shrinkage_slot,
):
    ny, nzh, nx, nzl = (lax.axis_size(a) for a in ("y", "zh", "x", "zl"))
    width = spectral_directions.shape[1]
    core = lax.axis_index("core")
    mine = core.reshape(1)
    y = lax.axis_index("y").reshape(1)

    swap = [(a * nzl + b, b * nzl + a) for a in range(nzh) for b in range(nzl)]
    signals = lax.ppermute(measured_signals.T, ("zh", "zl"), swap)
    given = lax.dynamic_slice_in_dim(spectral_directions, (1 - core) * (width // 2), width // 2, axis=1)
    half = hidden_states.shape[0] // 2
    kept = lax.dynamic_slice_in_dim(hidden_states, core * half, half)
    swapped = shift(lax.dynamic_slice_in_dim(hidden_states, (1 - core) * half, half), "core", 2, 1)
    features = jnp.stack([kept, swapped])
    signals, given, features = lax.optimization_barrier((signals, given, features))
    signals = gather(signals, "zl", nzl)
    features = [features] + [shift(features, "y", ny, k) for k in range(1, ny)]
    signals = gather(signals, "x", nx)
    signals, *features = lax.optimization_barrier((signals, *features))
    received = shift(cross_products(1, y, signals, features), "core", 2, 1)
    kept = cross_products(0, y, signals, features)
    cross = scaled(kept, received, nzh, 2 * half * ny * nzh)

    cross, given = lax.optimization_barrier((cross, given))
    their_directions = shift(given, "core", 2, 1)
    parts = exchange(cross.astype(F16), "zh").astype(F32)

    covariance = rounded_covariance(parts)
    covariances = lax.all_gather(covariance, "core", axis=0, tiled=False)
    rotated = rotate(mine, covariances, spectral_directions, their_directions, nx, nzl)
    rotated = exchange(rotated, "x")
    rotated = exchange(add_parts(rotated), "zl")
    index = (core * nx + lax.axis_index("x")) * nzl + lax.axis_index("zl")
    shrunk = shrink(
        index.reshape(1), rotated, spectral_strengths, shrinkage_strengths, chosen_shrinkage_slot
    )

    shrunk = gather(shrunk, "zl", nzl)
    shrunk = gather(shrunk, "x", nx).reshape(width // 2, -1)
    theirs = encode(jnp.zeros((1,), jnp.int32), their_directions, shrunk)
    received = shift(theirs, "core", 2, 1)
    return encode(mine, spectral_directions, shrunk) + received


def solution(mesh):
    fine = Mesh(mesh.devices.reshape(4, 4, 4, 4, 2), ("y", "zh", "x", "zl", "core"))
    vox, feat = ("y", "zh"), ("x", "zl", "core")
    return jax.shard_map(
        per_device,
        mesh=fine,
        in_specs=(P(vox, feat), P(feat, vox), P(feat, None), P(), P(), P(vox)),
        out_specs=P(feat, vox),
        check_vma=False,
    )
```

```python
import functools

import jax
import jax.numpy as jnp
from jax import lax
from jax.experimental import pallas as pl
from jax.experimental.pallas import tpu as pltpu
from jax.sharding import Mesh, PartitionSpec as P

F32, BF16, F16 = jnp.float32, jnp.bfloat16, jnp.float16
STEPS = (64, 32, 16, 8, 4, 2)
EXTRA = 8


def exchange(blocks, axis):
    return lax.all_to_all(blocks, axis, 0, 0, tiled=True)


def gather(block, axis, size):
    return exchange(jnp.broadcast_to(block[None], (size,) + block.shape), axis)


def shift(block, axis, size, by):
    return lax.ppermute(block, axis, [(i, (i + by) % size) for i in range(size)])


def whole(count):
    return [pl.BlockSpec(memory_space=pltpu.VMEM)] * count


def cross_kernel(ny, which, y, signals, *refs):
    features, out = refs[:ny], refs[ny]
    groups, voxels, block = signals.shape[1:]
    acc = None
    for k in range(ny):
        left = signals[lax.rem(y[0] - k + ny, ny)].reshape(groups * voxels, block)
        term = jnp.dot(left, features[k][which], preferred_element_type=F32)
        acc = term if acc is None else acc + term
    out[...] = acc


def cross_products(which, y, signals, features):
    ny, (_, block, rows) = len(features), features[0].shape
    _, groups, voxels, _ = signals.shape
    return pl.pallas_call(
        functools.partial(cross_kernel, ny, which),
        out_shape=jax.ShapeDtypeStruct((groups * voxels, rows), F32),
        in_specs=[pl.BlockSpec(memory_space=pltpu.SMEM)] + whole(1 + ny),
        out_specs=pl.BlockSpec(memory_space=pltpu.VMEM),
        compiler_params=pltpu.CompilerParams(vmem_limit_bytes=16 << 20),
        cost_estimate=pl.CostEstimate(
            flops=2 * ny * block * groups * voxels * rows, bytes_accessed=4 << 20, transcendentals=0
        ),
    )(y, signals, *features)


def scale_kernel(total_time, kept, received, out):
    groups, voxels = out.shape[0], out.shape[1] - EXTRA
    acc = (kept[...] + received[...]) * (1.0 / total_time)
    top = jnp.max(jnp.max(jnp.abs(acc), axis=0, keepdims=True), axis=1, keepdims=True)
    scale, exponent = jnp.ones_like(top), jnp.zeros_like(top)
    for step in STEPS:
        grown = scale * 2.0**step
        fits = top * grown < 2.0**14
        scale = jnp.where(fits, grown, scale)
        exponent = jnp.where(fits, exponent + step, exponent)
    out[:, :voxels, :] = (acc * scale).reshape(groups, voxels, -1)
    out[:, voxels:, :] = jnp.broadcast_to(exponent[None], (groups, EXTRA, acc.shape[1]))


def scaled(kept, received, groups, total_time):
    rows, width = kept.shape
    return pl.pallas_call(
        functools.partial(scale_kernel, total_time),
        out_shape=jax.ShapeDtypeStruct((groups, rows // groups + EXTRA, width), F32),
        in_specs=whole(2),
        out_specs=pl.BlockSpec(memory_space=pltpu.VMEM),
        compiler_params=pltpu.CompilerParams(vmem_limit_bytes=16 << 20),
        cost_estimate=pl.CostEstimate(
            flops=5 * kept.size, bytes_accessed=12 * kept.size, transcendentals=0
        ),
    )(kept, received)


def covariance_kernel(parts, out):
    voxels = out.shape[0]
    total = None
    for k in range(parts.shape[0]):
        exponent = parts[k, voxels : voxels + 1, :]
        scale = jnp.ones_like(exponent)
        for step in STEPS:
            holds = exponent >= step
            scale = jnp.where(holds, scale * 0.5**step, scale)
            exponent = jnp.where(holds, exponent - step, exponent)
        term = parts[k, :voxels, :] * scale
        total = term if total is None else total + term
    out[...] = total.astype(out.dtype)


def rounded_covariance(parts):
    count, rows, width = parts.shape
    return pl.pallas_call(
        covariance_kernel,
        out_shape=jax.ShapeDtypeStruct((rows - EXTRA, width), BF16),
        in_specs=whole(1),
        out_specs=pl.BlockSpec(memory_space=pltpu.VMEM),
        compiler_params=pltpu.CompilerParams(vmem_limit_bytes=16 << 20),
        cost_estimate=pl.CostEstimate(
            flops=2 * parts.size, bytes_accessed=4 * parts.size, transcendentals=0
        ),
    )(parts)


def rotate_kernel(half, covariances, directions, their_directions, out):
    own, theirs = covariances[half[0]], covariances[1 - half[0]]
    product = jnp.dot(own, directions[...], preferred_element_type=F32)
    product += jnp.dot(theirs, their_directions[...], preferred_element_type=F32)
    share = out.shape[-1]
    for j in range(out.shape[1]):
        out[0, j] = product[:, j * share : (j + 1) * share].astype(out.dtype)


def rotate(half, covariances, directions, their_directions, nx, nzl):
    _, voxels, rows = covariances.shape
    columns = their_directions.shape[1] // nx
    share = columns // nzl
    return pl.pallas_call(
        rotate_kernel,
        out_shape=jax.ShapeDtypeStruct((nx, nzl, voxels, share), BF16),
        grid_spec=pltpu.PrefetchScalarGridSpec(
            num_scalar_prefetch=1,
            grid=(nx,),
            in_specs=[
                pl.BlockSpec(covariances.shape, lambda i, h: (0, 0, 0)),
                pl.BlockSpec((rows, columns), lambda i, h: (0, h[0] * nx + i)),
                pl.BlockSpec((rows, columns), lambda i, h: (0, i)),
            ],
            out_specs=pl.BlockSpec((1, nzl, voxels, share), lambda i, h: (i, 0, 0, 0)),
        ),
        compiler_params=pltpu.CompilerParams(vmem_limit_bytes=16 << 20),
        cost_estimate=pl.CostEstimate(
            flops=4 * rows * columns * nx * voxels, bytes_accessed=4 << 20, transcendentals=0
        ),
    )(half, covariances, directions, their_directions)


def add_kernel(parts, out):
    out[...] = jnp.sum(parts[...].astype(F32), axis=0).astype(out.dtype)


def add_parts(parts):
    return pl.pallas_call(
        add_kernel,
        out_shape=jax.ShapeDtypeStruct(parts.shape[1:], BF16),
        in_specs=whole(1),
        out_specs=pl.BlockSpec(memory_space=pltpu.VMEM),
        compiler_params=pltpu.CompilerParams(vmem_limit_bytes=16 << 20),
        cost_estimate=pl.CostEstimate(
            flops=parts.size, bytes_accessed=3 * parts.size, transcendentals=0
        ),
    )(parts)


def shrink_kernel(levels, which, parts, strengths, slots, grid_values, out):
    voxels = slots.shape[1]
    ridge = jnp.zeros((1, voxels), F32)
    for level in range(levels):
        ridge = jnp.where(slots[...] == level, grid_values[level], ridge)
    column = jnp.broadcast_to(ridge, (voxels, voxels)).T
    rotated = jnp.sum(parts[...].astype(F32), axis=0)
    for j in range(0, out.shape[0], voxels):
        denominator = strengths[0, :, j : j + voxels] + column
        out[j : j + voxels, :] = (rotated[:, j : j + voxels] / denominator).T.astype(out.dtype)


def shrink(which, parts, strengths, grid_values, slots):
    _, voxels, share = parts.shape
    levels = grid_values.shape[0]
    return pl.pallas_call(
        functools.partial(shrink_kernel, levels),
        out_shape=jax.ShapeDtypeStruct((share, voxels), BF16),
        grid_spec=pltpu.PrefetchScalarGridSpec(
            num_scalar_prefetch=1,
            grid=(1,),
            in_specs=[
                pl.BlockSpec(parts.shape, lambda i, w: (0, 0, 0)),
                pl.BlockSpec((1, 1, share), lambda i, w: (w[0], 0, 0)),
                pl.BlockSpec((1, voxels), lambda i, w: (0, 0)),
                pl.BlockSpec(memory_space=pltpu.SMEM),
            ],
            out_specs=pl.BlockSpec((share, voxels), lambda i, w: (0, 0)),
        ),
        compiler_params=pltpu.CompilerParams(vmem_limit_bytes=16 << 20),
        cost_estimate=pl.CostEstimate(
            flops=6 * parts.size, bytes_accessed=2 * parts.size, transcendentals=0
        ),
    )(which, parts, strengths.reshape(-1, 1, share), slots.reshape(1, voxels), grid_values)


def encode_kernel(half, directions, shrunk, out):
    @pl.when(pl.program_id(0) == 0)
    def _():
        out[...] = jnp.zeros_like(out)

    out[...] += jnp.dot(directions[...], shrunk[...], preferred_element_type=F32)


def encode(half, directions, shrunk, steps=4):
    rows, _ = directions.shape
    depth, voxels = shrunk.shape
    columns = depth // steps
    return pl.pallas_call(
        encode_kernel,
        out_shape=jax.ShapeDtypeStruct((rows, voxels), F32),
        grid_spec=pltpu.PrefetchScalarGridSpec(
            num_scalar_prefetch=1,
            grid=(steps,),
            in_specs=[
                pl.BlockSpec((rows, columns), lambda i, h: (0, h[0] * steps + i)),
                pl.BlockSpec((columns, voxels), lambda i, h: (i, 0)),
            ],
            out_specs=pl.BlockSpec((rows, voxels), lambda i, h: (0, 0)),
        ),
        compiler_params=pltpu.CompilerParams(vmem_limit_bytes=16 << 20),
        cost_estimate=pl.CostEstimate(
            flops=2 * rows * depth * voxels, bytes_accessed=4 << 20, transcendentals=0
        ),
    )(half, directions, shrunk)


def per_device(
    hidden_states,
    measured_signals,
    spectral_directions,
    spectral_strengths,
    shrinkage_strengths,
    chosen_shrinkage_slot,
):
    ny, nzh, nx, nzl = (lax.axis_size(a) for a in ("y", "zh", "x", "zl"))
    width = spectral_directions.shape[1]
    core = lax.axis_index("core")
    mine = core.reshape(1)
    y = lax.axis_index("y").reshape(1)

    swap = [(a * nzl + b, b * nzl + a) for a in range(nzh) for b in range(nzl)]
    signals = lax.ppermute(measured_signals.T, ("zh", "zl"), swap)
    given = lax.dynamic_slice_in_dim(spectral_directions, (1 - core) * (width // 2), width // 2, axis=1)
    half = hidden_states.shape[0] // 2
    kept = lax.dynamic_slice_in_dim(hidden_states, core * half, half)
    swapped = shift(lax.dynamic_slice_in_dim(hidden_states, (1 - core) * half, half), "core", 2, 1)
    features = jnp.stack([kept, swapped])
    signals, given, features = lax.optimization_barrier((signals, given, features))
    features = [features] + [shift(features, "y", ny, k) for k in range(1, ny)]
    signals = gather(signals, ("x", "zl"), nx * nzl)
    signals = signals.reshape((nx, nzl) + signals.shape[1:])
    signals, *features = lax.optimization_barrier((signals, *features))
    received = shift(cross_products(1, y, signals, features), "core", 2, 1)
    kept = cross_products(0, y, signals, features)
    cross = scaled(kept, received, nzh, 2 * half * ny * nzh)

    cross, given = lax.optimization_barrier((cross, given))
    their_directions = shift(given, "core", 2, 1)
    parts = exchange(cross.astype(F16), "zh").astype(F32)

    covariance = rounded_covariance(parts)
    covariances = lax.all_gather(covariance, "core", axis=0, tiled=False)
    rotated = rotate(mine, covariances, spectral_directions, their_directions, nx, nzl)
    rotated = exchange(rotated, "x")
    rotated = exchange(add_parts(rotated), "zl")
    index = (core * nx + lax.axis_index("x")) * nzl + lax.axis_index("zl")
    shrunk = shrink(
        index.reshape(1), rotated, spectral_strengths, shrinkage_strengths, chosen_shrinkage_slot
    )

    shrunk = gather(shrunk, "zl", nzl)
    shrunk = gather(shrunk, "x", nx).reshape(width // 2, -1)
    theirs = encode(jnp.zeros((1,), jnp.int32), their_directions, shrunk)
    received = shift(theirs, "core", 2, 1)
    return encode(mine, spectral_directions, shrunk) + received


def solution(mesh):
    fine = Mesh(mesh.devices.reshape(4, 4, 4, 4, 2), ("y", "zh", "x", "zl", "core"))
    vox, feat = ("y", "zh"), ("x", "zl", "core")
    return jax.shard_map(
        per_device,
        mesh=fine,
        in_specs=(P(vox, feat), P(feat, vox), P(feat, None), P(), P(), P(vox)),
        out_specs=P(feat, vox),
        check_vma=False,
    )
```

```python
import functools

import jax
import jax.numpy as jnp
from jax import lax
from jax.experimental import pallas as pl
from jax.experimental.pallas import tpu as pltpu
from jax.sharding import Mesh, PartitionSpec as P

F32, BF16, F16 = jnp.float32, jnp.bfloat16, jnp.float16
STEPS = (64, 32, 16, 8, 4, 2)
EXTRA = 8


def exchange(blocks, axis):
    return lax.all_to_all(blocks, axis, 0, 0, tiled=True)


def gather(block, axis, size):
    return exchange(jnp.broadcast_to(block[None], (size,) + block.shape), axis)


def shift(block, axis, size, by):
    return lax.ppermute(block, axis, [(i, (i + by) % size) for i in range(size)])


def whole(count):
    return [pl.BlockSpec(memory_space=pltpu.VMEM)] * count


def cross_kernel(ny, which, y, signals, *refs):
    features, out = refs[:ny], refs[ny]
    groups, voxels, block = signals.shape[1:]
    acc = None
    for k in range(ny):
        left = signals[lax.rem(y[0] - k + ny, ny)].reshape(groups * voxels, block)
        term = jnp.dot(left, features[k][which], preferred_element_type=F32)
        acc = term if acc is None else acc + term
    out[...] = acc


def cross_products(which, y, signals, features):
    ny, (_, block, rows) = len(features), features[0].shape
    _, groups, voxels, _ = signals.shape
    return pl.pallas_call(
        functools.partial(cross_kernel, ny, which),
        out_shape=jax.ShapeDtypeStruct((groups * voxels, rows), F32),
        in_specs=[pl.BlockSpec(memory_space=pltpu.SMEM)] + whole(1 + ny),
        out_specs=pl.BlockSpec(memory_space=pltpu.VMEM),
        compiler_params=pltpu.CompilerParams(vmem_limit_bytes=16 << 20),
        cost_estimate=pl.CostEstimate(
            flops=2 * ny * block * groups * voxels * rows, bytes_accessed=4 << 20, transcendentals=0
        ),
    )(y, signals, *features)


def scale_kernel(total_time, kept, received, out):
    groups, voxels = out.shape[0], out.shape[1] - EXTRA
    acc = (kept[...] + received[...]) * (1.0 / total_time)
    top = jnp.max(jnp.max(jnp.abs(acc), axis=0, keepdims=True), axis=1, keepdims=True)
    scale, exponent = jnp.ones_like(top), jnp.zeros_like(top)
    for step in STEPS:
        grown = scale * 2.0**step
        fits = top * grown < 2.0**14
        scale = jnp.where(fits, grown, scale)
        exponent = jnp.where(fits, exponent + step, exponent)
    out[:, :voxels, :] = (acc * scale).reshape(groups, voxels, -1)
    out[:, voxels:, :] = jnp.broadcast_to(exponent[None], (groups, EXTRA, acc.shape[1]))


def scaled(kept, received, groups, total_time):
    rows, width = kept.shape
    return pl.pallas_call(
        functools.partial(scale_kernel, total_time),
        out_shape=jax.ShapeDtypeStruct((groups, rows // groups + EXTRA, width), F32),
        in_specs=whole(2),
        out_specs=pl.BlockSpec(memory_space=pltpu.VMEM),
        compiler_params=pltpu.CompilerParams(vmem_limit_bytes=16 << 20),
        cost_estimate=pl.CostEstimate(
            flops=5 * kept.size, bytes_accessed=12 * kept.size, transcendentals=0
        ),
    )(kept, received)


def covariance_kernel(parts, out):
    voxels = out.shape[0]
    total = None
    for k in range(parts.shape[0]):
        exponent = parts[k, voxels : voxels + 1, :]
        scale = jnp.ones_like(exponent)
        for step in STEPS:
            holds = exponent >= step
            scale = jnp.where(holds, scale * 0.5**step, scale)
            exponent = jnp.where(holds, exponent - step, exponent)
        term = parts[k, :voxels, :] * scale
        total = term if total is None else total + term
    out[...] = total.astype(out.dtype)


def rounded_covariance(parts):
    count, rows, width = parts.shape
    return pl.pallas_call(
        covariance_kernel,
        out_shape=jax.ShapeDtypeStruct((rows - EXTRA, width), BF16),
        in_specs=whole(1),
        out_specs=pl.BlockSpec(memory_space=pltpu.VMEM),
        compiler_params=pltpu.CompilerParams(vmem_limit_bytes=16 << 20),
        cost_estimate=pl.CostEstimate(
            flops=2 * parts.size, bytes_accessed=4 * parts.size, transcendentals=0
        ),
    )(parts)


def rotate_kernel(half, covariances, directions, their_directions, out):
    own, theirs = covariances[half[0]], covariances[1 - half[0]]
    product = jnp.dot(own, directions[...], preferred_element_type=F32)
    product += jnp.dot(theirs, their_directions[...], preferred_element_type=F32)
    share = out.shape[-1]
    for j in range(out.shape[1]):
        out[0, j] = product[:, j * share : (j + 1) * share].astype(out.dtype)


def rotate(half, covariances, directions, their_directions, nx, nzl):
    _, voxels, rows = covariances.shape
    columns = their_directions.shape[1] // nx
    share = columns // nzl
    return pl.pallas_call(
        rotate_kernel,
        out_shape=jax.ShapeDtypeStruct((nx, nzl, voxels, share), BF16),
        grid_spec=pltpu.PrefetchScalarGridSpec(
            num_scalar_prefetch=1,
            grid=(nx,),
            in_specs=[
                pl.BlockSpec(covariances.shape, lambda i, h: (0, 0, 0)),
                pl.BlockSpec((rows, columns), lambda i, h: (0, h[0] * nx + i)),
                pl.BlockSpec((rows, columns), lambda i, h: (0, i)),
            ],
            out_specs=pl.BlockSpec((1, nzl, voxels, share), lambda i, h: (i, 0, 0, 0)),
        ),
        compiler_params=pltpu.CompilerParams(vmem_limit_bytes=16 << 20),
        cost_estimate=pl.CostEstimate(
            flops=4 * rows * columns * nx * voxels, bytes_accessed=4 << 20, transcendentals=0
        ),
    )(half, covariances, directions, their_directions)


def add_kernel(parts, out):
    out[...] = jnp.sum(parts[...].astype(F32), axis=0).astype(out.dtype)


def add_parts(parts):
    return pl.pallas_call(
        add_kernel,
        out_shape=jax.ShapeDtypeStruct(parts.shape[1:], BF16),
        in_specs=whole(1),
        out_specs=pl.BlockSpec(memory_space=pltpu.VMEM),
        compiler_params=pltpu.CompilerParams(vmem_limit_bytes=16 << 20),
        cost_estimate=pl.CostEstimate(
            flops=parts.size, bytes_accessed=3 * parts.size, transcendentals=0
        ),
    )(parts)


def shrink_kernel(levels, which, parts, strengths, slots, grid_values, out):
    voxels = slots.shape[1]
    ridge = jnp.zeros((1, voxels), F32)
    for level in range(levels):
        ridge = jnp.where(slots[...] == level, grid_values[level], ridge)
    column = jnp.broadcast_to(ridge, (voxels, voxels)).T
    rotated = jnp.sum(parts[...].astype(F32), axis=0)
    for j in range(0, out.shape[0], voxels):
        denominator = strengths[0, :, j : j + voxels] + column
        out[j : j + voxels, :] = (rotated[:, j : j + voxels] / denominator).T.astype(out.dtype)


def shrink(which, parts, strengths, grid_values, slots):
    _, voxels, share = parts.shape
    levels = grid_values.shape[0]
    return pl.pallas_call(
        functools.partial(shrink_kernel, levels),
        out_shape=jax.ShapeDtypeStruct((share, voxels), BF16),
        grid_spec=pltpu.PrefetchScalarGridSpec(
            num_scalar_prefetch=1,
            grid=(1,),
            in_specs=[
                pl.BlockSpec(parts.shape, lambda i, w: (0, 0, 0)),
                pl.BlockSpec((1, 1, share), lambda i, w: (w[0], 0, 0)),
                pl.BlockSpec((1, voxels), lambda i, w: (0, 0)),
                pl.BlockSpec(memory_space=pltpu.SMEM),
            ],
            out_specs=pl.BlockSpec((share, voxels), lambda i, w: (0, 0)),
        ),
        compiler_params=pltpu.CompilerParams(vmem_limit_bytes=16 << 20),
        cost_estimate=pl.CostEstimate(
            flops=6 * parts.size, bytes_accessed=2 * parts.size, transcendentals=0
        ),
    )(which, parts, strengths.reshape(-1, 1, share), slots.reshape(1, voxels), grid_values)


def encode_kernel(half, directions, shrunk, out):
    @pl.when(pl.program_id(0) == 0)
    def _():
        out[...] = jnp.zeros_like(out)

    out[...] += jnp.dot(directions[...], shrunk[...], preferred_element_type=F32)


def encode(half, directions, shrunk, steps=4):
    rows, _ = directions.shape
    depth, voxels = shrunk.shape
    columns = depth // steps
    return pl.pallas_call(
        encode_kernel,
        out_shape=jax.ShapeDtypeStruct((rows, voxels), F32),
        grid_spec=pltpu.PrefetchScalarGridSpec(
            num_scalar_prefetch=1,
            grid=(steps,),
            in_specs=[
                pl.BlockSpec((rows, columns), lambda i, h: (0, h[0] * steps + i)),
                pl.BlockSpec((columns, voxels), lambda i, h: (i, 0)),
            ],
            out_specs=pl.BlockSpec((rows, voxels), lambda i, h: (0, 0)),
        ),
        compiler_params=pltpu.CompilerParams(vmem_limit_bytes=16 << 20),
        cost_estimate=pl.CostEstimate(
            flops=2 * rows * depth * voxels, bytes_accessed=4 << 20, transcendentals=0
        ),
    )(half, directions, shrunk)


def per_device(
    hidden_states,
    measured_signals,
    spectral_directions,
    spectral_strengths,
    shrinkage_strengths,
    chosen_shrinkage_slot,
):
    ny, nzh, nx, nzl = (lax.axis_size(a) for a in ("y", "zh", "x", "zl"))
    width = spectral_directions.shape[1]
    core = lax.axis_index("core")
    mine = core.reshape(1)
    y = lax.axis_index("y").reshape(1)

    swap = [(a * nzl + b, b * nzl + a) for a in range(nzh) for b in range(nzl)]
    signals = lax.ppermute(measured_signals.T, ("zh", "zl"), swap)
    given = lax.dynamic_slice_in_dim(spectral_directions, (1 - core) * (width // 2), width // 2, axis=1)
    half = hidden_states.shape[0] // 2
    kept = lax.dynamic_slice_in_dim(hidden_states, core * half, half)
    swapped = shift(lax.dynamic_slice_in_dim(hidden_states, (1 - core) * half, half), "core", 2, 1)
    features = jnp.stack([kept, swapped])
    signals, given, features = lax.optimization_barrier((signals, given, features))
    features = [features] + [shift(features, "y", ny, k) for k in range(1, ny)]
    signals = gather(signals, ("x", "zl"), nx * nzl)
    signals = signals.reshape((nx, nzl) + signals.shape[1:])
    signals, *features = lax.optimization_barrier((signals, *features))
    received = shift(cross_products(1, y, signals, features), "core", 2, 1)
    kept = cross_products(0, y, signals, features)
    cross = scaled(kept, received, nzh, 2 * half * ny * nzh)

    their_directions = shift(given, "core", 2, 1)
    parts = exchange(cross.astype(F16), "zh").astype(F32)

    covariance = rounded_covariance(parts)
    covariances = lax.all_gather(covariance, "core", axis=0, tiled=False)
    rotated = rotate(mine, covariances, spectral_directions, their_directions, nx, nzl)
    rotated = exchange(rotated, "x")
    rotated = exchange(add_parts(rotated), "zl")
    index = (core * nx + lax.axis_index("x")) * nzl + lax.axis_index("zl")
    shrunk = shrink(
        index.reshape(1), rotated, spectral_strengths, shrinkage_strengths, chosen_shrinkage_slot
    )

    shrunk = gather(shrunk, "zl", nzl)
    shrunk = gather(shrunk, "x", nx).reshape(width // 2, -1)
    theirs = encode(jnp.zeros((1,), jnp.int32), their_directions, shrunk)
    received = shift(theirs, "core", 2, 1)
    return encode(mine, spectral_directions, shrunk) + received


def solution(mesh):
    fine = Mesh(mesh.devices.reshape(4, 4, 4, 4, 2), ("y", "zh", "x", "zl", "core"))
    vox, feat = ("y", "zh"), ("x", "zl", "core")
    return jax.shard_map(
        per_device,
        mesh=fine,
        in_specs=(P(vox, feat), P(feat, vox), P(feat, None), P(), P(), P(vox)),
        out_specs=P(feat, vox),
        check_vma=False,
    )
```

```python
import functools

import jax
import jax.numpy as jnp
from jax import lax
from jax.experimental import pallas as pl
from jax.experimental.pallas import tpu as pltpu
from jax.sharding import Mesh, PartitionSpec as P

F32, BF16, F16 = jnp.float32, jnp.bfloat16, jnp.float16
STEPS = (64, 32, 16, 8, 4, 2)
EXTRA = 8


def exchange(blocks, axis):
    return lax.all_to_all(blocks, axis, 0, 0, tiled=True)


def gather(block, axis, size):
    return exchange(jnp.broadcast_to(block[None], (size,) + block.shape), axis)


def shift(block, axis, size, by):
    return lax.ppermute(block, axis, [(i, (i + by) % size) for i in range(size)])


def whole(count):
    return [pl.BlockSpec(memory_space=pltpu.VMEM)] * count


def cross_kernel(ny, which, y, signals, *refs):
    features, out = refs[:ny], refs[ny]
    groups, voxels, block = signals.shape[1:]
    acc = None
    for k in range(ny):
        left = signals[lax.rem(y[0] - k + ny, ny)].reshape(groups * voxels, block)
        term = jnp.dot(left, features[k][which], preferred_element_type=F32)
        acc = term if acc is None else acc + term
    out[...] = acc


def cross_products(which, y, signals, features):
    ny, (_, block, rows) = len(features), features[0].shape
    _, groups, voxels, _ = signals.shape
    return pl.pallas_call(
        functools.partial(cross_kernel, ny, which),
        out_shape=jax.ShapeDtypeStruct((groups * voxels, rows), F32),
        in_specs=[pl.BlockSpec(memory_space=pltpu.SMEM)] + whole(1 + ny),
        out_specs=pl.BlockSpec(memory_space=pltpu.VMEM),
        compiler_params=pltpu.CompilerParams(vmem_limit_bytes=16 << 20),
        cost_estimate=pl.CostEstimate(
            flops=2 * ny * block * groups * voxels * rows, bytes_accessed=4 << 20, transcendentals=0
        ),
    )(y, signals, *features)


def scale_kernel(total_time, kept, received, out):
    groups, voxels = out.shape[0], out.shape[1] - EXTRA
    acc = (kept[...] + received[...]) * (1.0 / total_time)
    top = jnp.max(jnp.max(jnp.abs(acc), axis=0, keepdims=True), axis=1, keepdims=True)
    scale, exponent = jnp.ones_like(top), jnp.zeros_like(top)
    for step in STEPS:
        grown = scale * 2.0**step
        fits = top * grown < 2.0**14
        scale = jnp.where(fits, grown, scale)
        exponent = jnp.where(fits, exponent + step, exponent)
    out[:, :voxels, :] = (acc * scale).reshape(groups, voxels, -1)
    out[:, voxels:, :] = jnp.broadcast_to(exponent[None], (groups, EXTRA, acc.shape[1]))


def scaled(kept, received, groups, total_time):
    rows, width = kept.shape
    return pl.pallas_call(
        functools.partial(scale_kernel, total_time),
        out_shape=jax.ShapeDtypeStruct((groups, rows // groups + EXTRA, width), F32),
        in_specs=whole(2),
        out_specs=pl.BlockSpec(memory_space=pltpu.VMEM),
        compiler_params=pltpu.CompilerParams(vmem_limit_bytes=16 << 20),
        cost_estimate=pl.CostEstimate(
            flops=5 * kept.size, bytes_accessed=12 * kept.size, transcendentals=0
        ),
    )(kept, received)


def covariance_kernel(parts, out):
    voxels = out.shape[0]
    total = None
    for k in range(parts.shape[0]):
        exponent = parts[k, voxels : voxels + 1, :]
        scale = jnp.ones_like(exponent)
        for step in STEPS:
            holds = exponent >= step
            scale = jnp.where(holds, scale * 0.5**step, scale)
            exponent = jnp.where(holds, exponent - step, exponent)
        term = parts[k, :voxels, :] * scale
        total = term if total is None else total + term
    out[...] = total.astype(out.dtype)


def rounded_covariance(parts):
    count, rows, width = parts.shape
    return pl.pallas_call(
        covariance_kernel,
        out_shape=jax.ShapeDtypeStruct((rows - EXTRA, width), BF16),
        in_specs=whole(1),
        out_specs=pl.BlockSpec(memory_space=pltpu.VMEM),
        compiler_params=pltpu.CompilerParams(vmem_limit_bytes=16 << 20),
        cost_estimate=pl.CostEstimate(
            flops=2 * parts.size, bytes_accessed=4 * parts.size, transcendentals=0
        ),
    )(parts)


def rotate_kernel(half, covariances, directions, their_directions, out):
    own, theirs = covariances[half[0]], covariances[1 - half[0]]
    product = jnp.dot(own, directions[...], preferred_element_type=F32)
    product += jnp.dot(theirs, their_directions[...], preferred_element_type=F32)
    share = out.shape[-1]
    for j in range(out.shape[1]):
        out[0, j] = product[:, j * share : (j + 1) * share].astype(out.dtype)


def rotate(half, covariances, directions, their_directions, nx, nzl):
    _, voxels, rows = covariances.shape
    columns = their_directions.shape[1] // nx
    share = columns // nzl
    return pl.pallas_call(
        rotate_kernel,
        out_shape=jax.ShapeDtypeStruct((nx, nzl, voxels, share), BF16),
        grid_spec=pltpu.PrefetchScalarGridSpec(
            num_scalar_prefetch=1,
            grid=(nx,),
            in_specs=[
                pl.BlockSpec(covariances.shape, lambda i, h: (0, 0, 0)),
                pl.BlockSpec((rows, columns), lambda i, h: (0, h[0] * nx + i)),
                pl.BlockSpec((rows, columns), lambda i, h: (0, i)),
            ],
            out_specs=pl.BlockSpec((1, nzl, voxels, share), lambda i, h: (i, 0, 0, 0)),
        ),
        compiler_params=pltpu.CompilerParams(vmem_limit_bytes=16 << 20),
        cost_estimate=pl.CostEstimate(
            flops=4 * rows * columns * nx * voxels, bytes_accessed=4 << 20, transcendentals=0
        ),
    )(half, covariances, directions, their_directions)


def add_kernel(parts, out):
    out[...] = jnp.sum(parts[...].astype(F32), axis=0).astype(out.dtype)


def add_parts(parts):
    return pl.pallas_call(
        add_kernel,
        out_shape=jax.ShapeDtypeStruct(parts.shape[1:], BF16),
        in_specs=whole(1),
        out_specs=pl.BlockSpec(memory_space=pltpu.VMEM),
        compiler_params=pltpu.CompilerParams(vmem_limit_bytes=16 << 20),
        cost_estimate=pl.CostEstimate(
            flops=parts.size, bytes_accessed=3 * parts.size, transcendentals=0
        ),
    )(parts)


def shrink_kernel(levels, which, parts, strengths, slots, grid_values, out):
    voxels = slots.shape[1]
    ridge = jnp.zeros((1, voxels), F32)
    for level in range(levels):
        ridge = jnp.where(slots[...] == level, grid_values[level], ridge)
    column = jnp.broadcast_to(ridge, (voxels, voxels)).T
    rotated = jnp.sum(parts[...].astype(F32), axis=0)
    for j in range(0, out.shape[0], voxels):
        denominator = strengths[0, :, j : j + voxels] + column
        out[j : j + voxels, :] = (rotated[:, j : j + voxels] / denominator).T.astype(out.dtype)


def shrink(which, parts, strengths, grid_values, slots):
    _, voxels, share = parts.shape
    levels = grid_values.shape[0]
    return pl.pallas_call(
        functools.partial(shrink_kernel, levels),
        out_shape=jax.ShapeDtypeStruct((share, voxels), BF16),
        grid_spec=pltpu.PrefetchScalarGridSpec(
            num_scalar_prefetch=1,
            grid=(1,),
            in_specs=[
                pl.BlockSpec(parts.shape, lambda i, w: (0, 0, 0)),
                pl.BlockSpec((1, 1, share), lambda i, w: (w[0], 0, 0)),
                pl.BlockSpec((1, voxels), lambda i, w: (0, 0)),
                pl.BlockSpec(memory_space=pltpu.SMEM),
            ],
            out_specs=pl.BlockSpec((share, voxels), lambda i, w: (0, 0)),
        ),
        compiler_params=pltpu.CompilerParams(vmem_limit_bytes=16 << 20),
        cost_estimate=pl.CostEstimate(
            flops=6 * parts.size, bytes_accessed=2 * parts.size, transcendentals=0
        ),
    )(which, parts, strengths.reshape(-1, 1, share), slots.reshape(1, voxels), grid_values)


def encode_kernel(half, directions, their_directions, shrunk, own, theirs):
    @pl.when(pl.program_id(0) == 0)
    def _():
        own[...] = jnp.zeros_like(own)
        theirs[...] = jnp.zeros_like(theirs)

    theirs[...] += jnp.dot(their_directions[...], shrunk[...], preferred_element_type=F32)
    own[...] += jnp.dot(directions[...], shrunk[...], preferred_element_type=F32)


def encode(half, directions, their_directions, shrunk, steps=4):
    rows, _ = directions.shape
    depth, voxels = shrunk.shape
    columns = depth // steps
    flat = pl.BlockSpec((rows, voxels), lambda i, h: (0, 0))
    return pl.pallas_call(
        encode_kernel,
        out_shape=[jax.ShapeDtypeStruct((rows, voxels), F32)] * 2,
        grid_spec=pltpu.PrefetchScalarGridSpec(
            num_scalar_prefetch=1,
            grid=(steps,),
            in_specs=[
                pl.BlockSpec((rows, columns), lambda i, h: (0, h[0] * steps + i)),
                pl.BlockSpec((rows, columns), lambda i, h: (0, i)),
                pl.BlockSpec((columns, voxels), lambda i, h: (i, 0)),
            ],
            out_specs=[flat, flat],
        ),
        compiler_params=pltpu.CompilerParams(vmem_limit_bytes=16 << 20),
        cost_estimate=pl.CostEstimate(
            flops=4 * rows * depth * voxels, bytes_accessed=4 << 20, transcendentals=0
        ),
    )(half, directions, their_directions, shrunk)


def per_device(
    hidden_states,
    measured_signals,
    spectral_directions,
    spectral_strengths,
    shrinkage_strengths,
    chosen_shrinkage_slot,
):
    ny, nzh, nx, nzl = (lax.axis_size(a) for a in ("y", "zh", "x", "zl"))
    width = spectral_directions.shape[1]
    core = lax.axis_index("core")
    mine = core.reshape(1)
    y = lax.axis_index("y").reshape(1)

    swap = [(a * nzl + b, b * nzl + a) for a in range(nzh) for b in range(nzl)]
    signals = lax.ppermute(measured_signals.T, ("zh", "zl"), swap)
    given = lax.dynamic_slice_in_dim(spectral_directions, (1 - core) * (width // 2), width // 2, axis=1)
    half = hidden_states.shape[0] // 2
    kept = lax.dynamic_slice_in_dim(hidden_states, core * half, half)
    swapped = shift(lax.dynamic_slice_in_dim(hidden_states, (1 - core) * half, half), "core", 2, 1)
    features = jnp.stack([kept, swapped])
    signals, given, features = lax.optimization_barrier((signals, given, features))
    features = [features] + [shift(features, "y", ny, k) for k in range(1, ny)]
    signals = gather(signals, ("x", "zl"), nx * nzl)
    signals = signals.reshape((nx, nzl) + signals.shape[1:])
    signals, *features = lax.optimization_barrier((signals, *features))
    received = shift(cross_products(1, y, signals, features), "core", 2, 1)
    kept = cross_products(0, y, signals, features)
    cross = scaled(kept, received, nzh, 2 * half * ny * nzh)

    their_directions = shift(given, "core", 2, 1)
    parts = exchange(cross.astype(F16), "zh").astype(F32)

    covariance = rounded_covariance(parts)
    covariances = lax.all_gather(covariance, "core", axis=0, tiled=False)
    rotated = rotate(mine, covariances, spectral_directions, their_directions, nx, nzl)
    rotated = exchange(rotated, "x")
    rotated = exchange(add_parts(rotated), "zl")
    index = (core * nx + lax.axis_index("x")) * nzl + lax.axis_index("zl")
    shrunk = shrink(
        index.reshape(1), rotated, spectral_strengths, shrinkage_strengths, chosen_shrinkage_slot
    )

    shrunk = gather(shrunk, "zl", nzl)
    shrunk = gather(shrunk, "x", nx).reshape(width // 2, -1)
    own, theirs = encode(mine, spectral_directions, their_directions, shrunk)
    theirs = lax.all_gather(theirs, "core", axis=0, tiled=False)
    return own + lax.dynamic_index_in_dim(theirs, 1 - core, 0, keepdims=False)


def solution(mesh):
    fine = Mesh(mesh.devices.reshape(4, 4, 4, 4, 2), ("y", "zh", "x", "zl", "core"))
    vox, feat = ("y", "zh"), ("x", "zl", "core")
    return jax.shard_map(
        per_device,
        mesh=fine,
        in_specs=(P(vox, feat), P(feat, vox), P(feat, None), P(), P(), P(vox)),
        out_specs=P(feat, vox),
        check_vma=False,
    )
```

```python
import functools

import jax
import jax.numpy as jnp
from jax import lax
from jax.experimental import pallas as pl
from jax.experimental.pallas import tpu as pltpu
from jax.sharding import Mesh, PartitionSpec as P

F32, BF16, F16 = jnp.float32, jnp.bfloat16, jnp.float16
STEPS = (64, 32, 16, 8, 4, 2)
EXTRA = 8


def exchange(blocks, axis):
    return lax.all_to_all(blocks, axis, 0, 0, tiled=True)


def gather(block, axis, size):
    return exchange(jnp.broadcast_to(block[None], (size,) + block.shape), axis)


def shift(block, axis, size, by):
    return lax.ppermute(block, axis, [(i, (i + by) % size) for i in range(size)])


def whole(count):
    return [pl.BlockSpec(memory_space=pltpu.VMEM)] * count


def cross_kernel(ny, which, y, signals, *refs):
    features, out = refs[:ny], refs[ny]
    groups, voxels, block = signals.shape[1:]
    acc = None
    for k in range(ny):
        left = signals[lax.rem(y[0] - k + ny, ny)].reshape(groups * voxels, block)
        term = jnp.dot(left, features[k][which], preferred_element_type=F32)
        acc = term if acc is None else acc + term
    out[...] = acc


def cross_products(which, y, signals, features):
    ny, (_, block, rows) = len(features), features[0].shape
    _, groups, voxels, _ = signals.shape
    return pl.pallas_call(
        functools.partial(cross_kernel, ny, which),
        out_shape=jax.ShapeDtypeStruct((groups * voxels, rows), F32),
        in_specs=[pl.BlockSpec(memory_space=pltpu.SMEM)] + whole(1 + ny),
        out_specs=pl.BlockSpec(memory_space=pltpu.VMEM),
        compiler_params=pltpu.CompilerParams(vmem_limit_bytes=16 << 20),
        cost_estimate=pl.CostEstimate(
            flops=2 * ny * block * groups * voxels * rows, bytes_accessed=4 << 20, transcendentals=0
        ),
    )(y, signals, *features)


def scale_kernel(total_time, kept, received, out):
    groups, voxels = out.shape[0], out.shape[1] - EXTRA
    acc = (kept[...] + received[...]) * (1.0 / total_time)
    top = jnp.max(jnp.max(jnp.abs(acc), axis=0, keepdims=True), axis=1, keepdims=True)
    scale, exponent = jnp.ones_like(top), jnp.zeros_like(top)
    for step in STEPS:
        grown = scale * 2.0**step
        fits = top * grown < 2.0**14
        scale = jnp.where(fits, grown, scale)
        exponent = jnp.where(fits, exponent + step, exponent)
    out[:, :voxels, :] = (acc * scale).reshape(groups, voxels, -1)
    out[:, voxels:, :] = jnp.broadcast_to(exponent[None], (groups, EXTRA, acc.shape[1]))


def scaled(kept, received, groups, total_time):
    rows, width = kept.shape
    return pl.pallas_call(
        functools.partial(scale_kernel, total_time),
        out_shape=jax.ShapeDtypeStruct((groups, rows // groups + EXTRA, width), F32),
        in_specs=whole(2),
        out_specs=pl.BlockSpec(memory_space=pltpu.VMEM),
        compiler_params=pltpu.CompilerParams(vmem_limit_bytes=16 << 20),
        cost_estimate=pl.CostEstimate(
            flops=5 * kept.size, bytes_accessed=12 * kept.size, transcendentals=0
        ),
    )(kept, received)


def covariance_kernel(parts, out):
    voxels = out.shape[0]
    total = None
    for k in range(parts.shape[0]):
        exponent = parts[k, voxels : voxels + 1, :]
        scale = jnp.ones_like(exponent)
        for step in STEPS:
            holds = exponent >= step
            scale = jnp.where(holds, scale * 0.5**step, scale)
            exponent = jnp.where(holds, exponent - step, exponent)
        term = parts[k, :voxels, :] * scale
        total = term if total is None else total + term
    out[...] = total.astype(out.dtype)


def rounded_covariance(parts):
    count, rows, width = parts.shape
    return pl.pallas_call(
        covariance_kernel,
        out_shape=jax.ShapeDtypeStruct((rows - EXTRA, width), BF16),
        in_specs=whole(1),
        out_specs=pl.BlockSpec(memory_space=pltpu.VMEM),
        compiler_params=pltpu.CompilerParams(vmem_limit_bytes=16 << 20),
        cost_estimate=pl.CostEstimate(
            flops=2 * parts.size, bytes_accessed=4 * parts.size, transcendentals=0
        ),
    )(parts)


def rotate_kernel(half, covariances, directions, their_directions, out):
    own, theirs = covariances[half[0]], covariances[1 - half[0]]
    product = jnp.dot(own, directions[...], preferred_element_type=F32)
    product += jnp.dot(theirs, their_directions[...], preferred_element_type=F32)
    share = out.shape[-1]
    for j in range(out.shape[1]):
        out[0, j] = product[:, j * share : (j + 1) * share].astype(out.dtype)


def rotate(half, covariances, directions, their_directions, nx, nzl):
    _, voxels, rows = covariances.shape
    columns = their_directions.shape[1] // nx
    share = columns // nzl
    return pl.pallas_call(
        rotate_kernel,
        out_shape=jax.ShapeDtypeStruct((nx, nzl, voxels, share), BF16),
        grid_spec=pltpu.PrefetchScalarGridSpec(
            num_scalar_prefetch=1,
            grid=(nx,),
            in_specs=[
                pl.BlockSpec(covariances.shape, lambda i, h: (0, 0, 0)),
                pl.BlockSpec((rows, columns), lambda i, h: (0, h[0] * nx + i)),
                pl.BlockSpec((rows, columns), lambda i, h: (0, i)),
            ],
            out_specs=pl.BlockSpec((1, nzl, voxels, share), lambda i, h: (i, 0, 0, 0)),
        ),
        compiler_params=pltpu.CompilerParams(vmem_limit_bytes=16 << 20),
        cost_estimate=pl.CostEstimate(
            flops=4 * rows * columns * nx * voxels, bytes_accessed=4 << 20, transcendentals=0
        ),
    )(half, covariances, directions, their_directions)


def add_kernel(parts, out):
    out[...] = jnp.sum(parts[...].astype(F32), axis=0).astype(out.dtype)


def add_parts(parts):
    return pl.pallas_call(
        add_kernel,
        out_shape=jax.ShapeDtypeStruct(parts.shape[1:], BF16),
        in_specs=whole(1),
        out_specs=pl.BlockSpec(memory_space=pltpu.VMEM),
        compiler_params=pltpu.CompilerParams(vmem_limit_bytes=16 << 20),
        cost_estimate=pl.CostEstimate(
            flops=parts.size, bytes_accessed=3 * parts.size, transcendentals=0
        ),
    )(parts)


def shrink_kernel(levels, which, parts, strengths, slots, grid_values, out):
    voxels = slots.shape[1]
    ridge = jnp.zeros((1, voxels), F32)
    for level in range(levels):
        ridge = jnp.where(slots[...] == level, grid_values[level], ridge)
    column = jnp.broadcast_to(ridge, (voxels, voxels)).T
    rotated = jnp.sum(parts[...].astype(F32), axis=0)
    for j in range(0, out.shape[0], voxels):
        denominator = strengths[0, :, j : j + voxels] + column
        out[j : j + voxels, :] = (rotated[:, j : j + voxels] / denominator).T.astype(out.dtype)


def shrink(which, parts, strengths, grid_values, slots):
    _, voxels, share = parts.shape
    levels = grid_values.shape[0]
    return pl.pallas_call(
        functools.partial(shrink_kernel, levels),
        out_shape=jax.ShapeDtypeStruct((share, voxels), BF16),
        grid_spec=pltpu.PrefetchScalarGridSpec(
            num_scalar_prefetch=1,
            grid=(1,),
            in_specs=[
                pl.BlockSpec(parts.shape, lambda i, w: (0, 0, 0)),
                pl.BlockSpec((1, 1, share), lambda i, w: (w[0], 0, 0)),
                pl.BlockSpec((1, voxels), lambda i, w: (0, 0)),
                pl.BlockSpec(memory_space=pltpu.SMEM),
            ],
            out_specs=pl.BlockSpec((share, voxels), lambda i, w: (0, 0)),
        ),
        compiler_params=pltpu.CompilerParams(vmem_limit_bytes=16 << 20),
        cost_estimate=pl.CostEstimate(
            flops=6 * parts.size, bytes_accessed=2 * parts.size, transcendentals=0
        ),
    )(which, parts, strengths.reshape(-1, 1, share), slots.reshape(1, voxels), grid_values)


def encode_kernel(first, half, directions, shrunk, *refs):
    out = refs[-1]

    @pl.when(pl.program_id(0) == 0)
    def _():
        out[...] = jnp.zeros_like(out) if first else refs[0][...]

    out[...] += jnp.dot(directions[...], shrunk[...], preferred_element_type=F32)


def encode(half, directions, shrunk, total=None, steps=4):
    rows, _ = directions.shape
    depth, voxels = shrunk.shape
    columns = depth // steps
    first = total is None
    flat = pl.BlockSpec((rows, voxels), lambda i, h: (0, 0))
    return pl.pallas_call(
        functools.partial(encode_kernel, first),
        out_shape=jax.ShapeDtypeStruct((rows, voxels), F32),
        grid_spec=pltpu.PrefetchScalarGridSpec(
            num_scalar_prefetch=1,
            grid=(steps,),
            in_specs=[
                pl.BlockSpec((rows, columns), lambda i, h: (0, h[0] * steps + i)),
                pl.BlockSpec((columns, voxels), lambda i, h: (i, 0)),
            ]
            + ([] if first else [flat]),
            out_specs=flat,
        ),
        compiler_params=pltpu.CompilerParams(vmem_limit_bytes=16 << 20),
        cost_estimate=pl.CostEstimate(
            flops=2 * rows * depth * voxels, bytes_accessed=4 << 20, transcendentals=0
        ),
    )(half, directions, shrunk, *([] if first else [total]))


def per_device(
    hidden_states,
    measured_signals,
    spectral_directions,
    spectral_strengths,
    shrinkage_strengths,
    chosen_shrinkage_slot,
):
    ny, nzh, nx, nzl = (lax.axis_size(a) for a in ("y", "zh", "x", "zl"))
    width = spectral_directions.shape[1]
    core = lax.axis_index("core")
    mine = core.reshape(1)
    y = lax.axis_index("y").reshape(1)

    swap = [(a * nzl + b, b * nzl + a) for a in range(nzh) for b in range(nzl)]
    signals = lax.ppermute(measured_signals.T, ("zh", "zl"), swap)
    given = lax.dynamic_slice_in_dim(spectral_directions, (1 - core) * (width // 2), width // 2, axis=1)
    half = hidden_states.shape[0] // 2
    kept = lax.dynamic_slice_in_dim(hidden_states, core * half, half)
    swapped = shift(lax.dynamic_slice_in_dim(hidden_states, (1 - core) * half, half), "core", 2, 1)
    features = jnp.stack([kept, swapped])
    signals, given, features = lax.optimization_barrier((signals, given, features))
    features = [features] + [shift(features, "y", ny, k) for k in range(1, ny)]
    signals = gather(signals, ("x", "zl"), nx * nzl)
    signals = signals.reshape((nx, nzl) + signals.shape[1:])
    signals, *features = lax.optimization_barrier((signals, *features))
    received = shift(cross_products(1, y, signals, features), "core", 2, 1)
    kept = cross_products(0, y, signals, features)
    cross = scaled(kept, received, nzh, 2 * half * ny * nzh)

    their_directions = shift(given, "core", 2, 1)
    parts = exchange(cross.astype(F16), "zh").astype(F32)

    covariance = rounded_covariance(parts)
    covariances = lax.all_gather(covariance, "core", axis=0, tiled=False)
    rotated = rotate(mine, covariances, spectral_directions, their_directions, nx, nzl)
    rotated = exchange(rotated, "x")
    rotated = exchange(add_parts(rotated), "zl")
    index = (core * nx + lax.axis_index("x")) * nzl + lax.axis_index("zl")
    shrunk = shrink(
        index.reshape(1), rotated, spectral_strengths, shrinkage_strengths, chosen_shrinkage_slot
    )

    shrunk = gather(shrunk, "zl", nzl)
    shrunk = gather(shrunk, "x", nx).reshape(width // 2, -1)
    theirs = encode(jnp.zeros((1,), jnp.int32), their_directions, shrunk)
    received = shift(theirs, "core", 2, 1)
    return encode(mine, spectral_directions, shrunk, received)


def solution(mesh):
    fine = Mesh(mesh.devices.reshape(4, 4, 4, 4, 2), ("y", "zh", "x", "zl", "core"))
    vox, feat = ("y", "zh"), ("x", "zl", "core")
    return jax.shard_map(
        per_device,
        mesh=fine,
        in_specs=(P(vox, feat), P(feat, vox), P(feat, None), P(), P(), P(vox)),
        out_specs=P(feat, vox),
        check_vma=False,
    )
```
